32 devices in a mesh: groups: 2 (over x), node: 16 (over z, y, core).
Axes of the slice: x: 2, y: 2, z: 4, core: 2. Of those that a mesh axis runs over, the one named last changes fastest.
Arguments:
- features: bfloat16 [262144, 128], P(('groups', 'node')), parts along dimension 0, may hold values from -6 to 6
- neighbors: int32 [262144, 16], P(('groups', 'node')), parts along dimension 0, may hold values from 0 to 10367
- degree: int32 [262144], P(('groups', 'node')), parts along dimension 0, may hold values from 1 to 16
- send_list: int32 [32, 16, 128], P(('groups', 'node')), parts along dimension 0, may hold values from 0 to 8191
- hub_rows: int32 [32, 8], P(('groups', 'node')), parts along dimension 0, may hold values from 0 to 8191
- w_self: bfloat16 [128, 128], replicated, may hold values from -0.5 to 0.5
- w_neigh: bfloat16 [128, 128], replicated, may hold values from -0.5 to 0.5
- bias: float32 [128], replicated, may hold values from -3 to 3
Outputs:
- hidden_out: bfloat16 [262144, 128], P(('groups', 'node')), parts along dimension 0
The draws below stay inside these ranges and needn't reach their ends.
There are 2 independent parts, one for each index of `groups`. The reference program is written for one: setup_inputs(seed, part) draws one part's arguments, and reference() takes and returns one part's arrays. A program takes and returns all parts, laid end to end along the dimension named above; an argument that names none is the same for every part. Nothing has to cross between parts.
All inputs are finite; a program needn't handle non-finite values.
Results may differ from the reference program's by a relative error of at most 0.0026.
Values may be sent and summed in bfloat16 or wider, within the bound.
No kernel may reach another device: no remote copies, remote signals or barrier semaphores. Data moves between devices by JAX's collectives and lax.ppermute only.
A program may use at most 128 MiB of HBM per device.

```python
import jax
import jax.numpy as jnp
from jax import lax

F = 128
NODE_DEV = 8192
K = 16
C = 128
HUB = 8
NODES = 131072
TABLE = 10368
N_NODE = 16


def place_ends(drawn, own_key, smallest, top_value):
    longest = drawn.shape.index(max(drawn.shape))
    spots = []
    for shift in (0, 1):
        where = [jax.random.randint(jax.random.fold_in(own_key, axis), (), 0, length) for axis, length in enumerate(drawn.shape)]
        where[longest] = (where[longest] + shift) % drawn.shape[longest]
        spots.append(tuple(where))
    return drawn.at[spots[0]].set(smallest).at[spots[1]].set(top_value)


def steps_of(rng, dims, split, least, top_value):
    def one(position, blocks):
        steps = jax.random.uniform(jax.random.fold_in(jax.random.fold_in(rng, 6), position), (blocks,), jnp.float32, least / len(split), top_value / len(split))
        return jnp.repeat(jnp.exp(steps), dims[position] // blocks).reshape((-1,) + (1,) * (len(dims) - position - 1))

    level = one(*split[0])
    for cut in split[1:]:
        level = level * one(*cut)
    return level


def gaussian(stream_key, dims, width, most, split=(), kind=jnp.bfloat16):
    drawn = width * jax.random.normal(stream_key, dims, jnp.float32)
    if split:
        drawn = drawn * steps_of(stream_key, dims, split, -0.22, 0.18)
    return jnp.clip(drawn, -most, most).astype(kind)


def setup_inputs(seed: int = 0, part: int = 0) -> dict:
    splits = jax.random.split(jax.random.key(seed), 9)
    part_splits = jax.random.split(jax.random.fold_in(splits[8], part), 9)
    features = gaussian(part_splits[0], (NODES, F), 1.0, 6.0, ((0, 16),))
    neighbors = place_ends(jax.random.randint(part_splits[1], (NODES, K), 0, TABLE), jax.random.fold_in(part_splits[1], 1), 0, TABLE - 1).astype(jnp.int32)
    degree = place_ends(jax.random.randint(part_splits[2], (NODES,), 1, K + 1), jax.random.fold_in(part_splits[2], 1), 1, K).astype(jnp.int32)
    send_list = place_ends(jax.random.randint(part_splits[3], (N_NODE, N_NODE, C), 0, NODE_DEV), jax.random.fold_in(part_splits[3], 1), 0, NODE_DEV - 1).astype(jnp.int32)
    hub_rows = place_ends(jax.random.randint(part_splits[4], (N_NODE, HUB), 0, NODE_DEV), jax.random.fold_in(part_splits[4], 1), 0, NODE_DEV - 1).astype(jnp.int32)
    w_self = gaussian(splits[5], (F, F), F ** -0.5, 0.5)
    w_neigh = gaussian(splits[6], (F, F), F ** -0.5, 0.5)
    bias = gaussian(splits[7], (F,), 0.5, 3.0, (), jnp.float32)
    return {"features": features, "neighbors": neighbors, "degree": degree, "send_list": send_list, "hub_rows": hub_rows, "w_self": w_self, "w_neigh": w_neigh, "bias": bias}


def reference(features, neighbors, degree, send_list, hub_rows, w_self, w_neigh, bias):
    per_dev = features.reshape(N_NODE, NODE_DEV, F)
    sources = jnp.arange(N_NODE, dtype=jnp.int32)[:, None]
    hubs = per_dev[sources, hub_rows].reshape(N_NODE * HUB, F)

    def one_device(items):
        dev, own, nbrs, degs = items
        halo = per_dev[sources, send_list[:, dev, :]].reshape(N_NODE * C, F)
        table = jnp.concatenate([own, halo, hubs], axis=0)
        rows = jnp.take(table, nbrs, axis=0).astype(jnp.float32)
        mask = (jnp.arange(K, dtype=jnp.int32)[None, :] < degs[:, None]).astype(jnp.float32)
        total = jnp.einsum("nk,nkf->nf", mask, rows)
        aggregate = (total / degs[:, None].astype(jnp.float32)).astype(jnp.bfloat16)
        mixed = jnp.dot(own, w_self, preferred_element_type=jnp.float32)
        mixed = mixed + jnp.dot(aggregate, w_neigh, preferred_element_type=jnp.float32) + bias
        return jnp.maximum(mixed, 0.0).astype(jnp.bfloat16)

    result = lax.map(one_device, (jnp.arange(N_NODE, dtype=jnp.int32), per_dev, neighbors.reshape(N_NODE, NODE_DEV, K), degree.reshape(N_NODE, NODE_DEV)))
    return result.reshape(NODES, F)
```

```python
import functools

import jax
import jax.numpy as jnp
from jax import lax
from jax.experimental import pallas as pl
from jax.experimental.pallas import tpu as pltpu
from jax.sharding import PartitionSpec as P

F8 = jnp.float8_e4m3fn
BF16 = jnp.bfloat16
F32 = jnp.float32
LO = 256
VMEM_BYTES = 56 * 2**20


def outgoing_kernel(send_ref, hub_ref, feat_ref, out_ref, wide, picked, *, peers, rows, hubs, block):
    nodes = feat_ref.shape[0]

    @pl.loop(0, nodes // 256)
    def _(step):
        at = pl.ds(pl.multiple_of(step * 256, 256), 256)
        wide[at, :] = feat_ref[at, :].astype(F32)

    picked[...] = jnp.zeros_like(picked)
    for j in range(hubs):
        picked[rows + j : rows + j + 1, :] = wide[pl.ds(hub_ref[j], 1), :]

    @pl.loop(0, peers)
    def _(peer):
        for c in range(rows):
            picked[c : c + 1, :] = wide[pl.ds(send_ref[peer * rows + c], 1), :]
        at = pl.ds(pl.multiple_of(peer * block, 16), block)
        out_ref[at, :] = picked[...].astype(BF16)


def split(values):
    scaled = values.astype(F32) * 64.0
    high = scaled.astype(F8)
    low = ((scaled - high.astype(F32)) * 16.0).astype(F8)
    return high, low


def count_tile(row, group, highs):
    lanes = row.shape[1]
    per = lanes // group
    high = lax.shift_right_arithmetic(row, 8)
    low = row & (LO - 1)
    lane_node = lax.broadcasted_iota(jnp.int32, (2 * group, lanes), 1) // per
    sub = lax.broadcasted_iota(jnp.int32, (2 * group, lanes), 0)
    mine = jnp.where(lane_node == sub % group, jnp.broadcast_to(high, (2 * group, lanes)) - sub // group, -100).astype(jnp.int8)
    one = jnp.ones((2 * group, lanes), F8)
    zero = jnp.zeros((2 * group, lanes), F8)
    left = jnp.concatenate([jnp.where(mine == jnp.int8(2 * j), one, zero) for j in range(highs // 2)], axis=0)
    lows = jnp.broadcast_to(low - 128, (32, lanes)).astype(jnp.int8)
    sub = lax.broadcasted_iota(jnp.int32, (32, lanes), 0)
    one = jnp.ones((32, lanes), F8)
    zero = jnp.zeros((32, lanes), F8)
    right = jnp.concatenate(
        [jnp.where(lows == (sub + (32 * j - 128)).astype(jnp.int8), one, zero) for j in range(LO // 32)], axis=0
    )
    counts = lax.dot_general(left, right, (((1,), (1,)), ((), ())), preferred_element_type=F32)
    return counts.reshape(highs, group, LO)


def layer_kernel(
    index_ref, degree_ref, feat_ref, halo_ref, self_ref, neigh_ref, bias_ref, out_ref, table, counts, hub_rows, *, tile, group, peers, rows, hubs, block, highs, unroll
):
    nodes, width = feat_ref.shape
    step = pl.program_id(0)

    def put(at, size, values):
        high, low = split(values)
        table[pl.ds(at, size), :width] = high
        table[pl.ds(at, size), width:] = low

    @pl.when(step == 0)
    def _():
        @pl.loop(0, nodes // 256)
        def _(i):
            at = pl.multiple_of(i * 256, 256)
            put(at, 256, feat_ref[pl.ds(at, 256), :])

        hub_rows[...] = jnp.zeros_like(hub_rows)

        @pl.loop(0, peers)
        def _(i):
            at = pl.multiple_of(i * block, 16)
            put(pl.multiple_of(nodes + i * rows, 32), rows, halo_ref[pl.ds(at, rows), :])
            tail = halo_ref[pl.ds(at + rows, block - rows), :].astype(F32)
            hub_rows[pl.ds(pl.multiple_of(i * hubs, 8), hubs), :] = tail[:hubs, :]

        put(nodes + peers * rows, hub_rows.shape[0], hub_rows[...])

    def pair(i, carry):
        both = [count_tile(index_ref[pl.ds(2 * i + j, 1), :], group, highs) for j in range(2)]
        both = jnp.concatenate(both, axis=1).astype(F8)
        at = pl.ds(pl.multiple_of(i * 2 * group, 2 * group), 2 * group)
        for h in range(highs):
            counts[at, h * LO : (h + 1) * LO] = both[h]
        return carry

    lax.fori_loop(0, tile // (2 * group), pair, 0, unroll=unroll)
    total = jnp.dot(counts[...], table[...], preferred_element_type=F32)
    total = total[:, :width] * (1.0 / 64.0) + total[:, width:] * (1.0 / 1024.0)
    eye = lax.broadcasted_iota(jnp.int32, (128, 128), 0) == lax.broadcasted_iota(jnp.int32, (128, 128), 1)
    ones = jnp.ones((128, width), BF16)
    spread = []
    for j in range(tile // 128):
        line = degree_ref[pl.ds(step * (tile // 128) + j, 1), :].astype(F32)
        spread.append(jnp.dot(jnp.where(eye, line, 0.0).astype(BF16), ones, preferred_element_type=F32))
    aggregate = (total / jnp.concatenate(spread, axis=0)).astype(BF16)
    own = feat_ref[pl.ds(pl.multiple_of(step * tile, tile), tile), :]
    mixed = jnp.dot(own, self_ref[...], preferred_element_type=F32)
    mixed = mixed + jnp.dot(aggregate, neigh_ref[...], preferred_element_type=F32) + bias_ref[...]
    out_ref[...] = jnp.maximum(mixed, 0.0).astype(BF16)


def local(features, neighbors, degree, send_list, hub_rows, w_self, w_neigh, bias):
    nodes, width = features.shape
    fanout = neighbors.shape[1]
    _, peers, rows = send_list.shape
    hubs = hub_rows.shape[1]
    block = -(-(rows + hubs) // 16) * 16
    group = 256 // fanout
    highs = -(-(nodes + peers * (rows + hubs)) // (2 * LO)) * 2
    hub_space = highs * LO - nodes - peers * rows
    tile = 512
    smem = pl.BlockSpec(memory_space=pltpu.SMEM)
    vmem = pl.BlockSpec(memory_space=pltpu.VMEM)

    outgoing = pl.pallas_call(
        functools.partial(outgoing_kernel, peers=peers, rows=rows, hubs=hubs, block=block),
        in_specs=[smem, smem, vmem],
        out_specs=vmem,
        out_shape=jax.ShapeDtypeStruct((peers * block, width), BF16),
        scratch_shapes=[pltpu.VMEM((nodes, width), F32), pltpu.VMEM((block, width), F32)],
        compiler_params=pltpu.CompilerParams(vmem_limit_bytes=VMEM_BYTES),
        name="outgoing_rows",
    )(send_list.reshape(-1), hub_rows.reshape(-1), features)
    halo = lax.all_to_all(outgoing.reshape(peers, block, width), "node", split_axis=0, concat_axis=0, tiled=True)
    halo = halo.reshape(peers * block, width)

    slots = lax.broadcasted_iota(jnp.int32, (nodes, fanout), 1)
    index = jnp.where(slots < degree[:, None], neighbors, -1).reshape(nodes // group, group * fanout)
    kernel = functools.partial(
        layer_kernel, tile=tile, group=group, peers=peers, rows=rows, hubs=hubs, block=block, highs=highs, unroll=8
    )
    whole = lambda *shape: pl.BlockSpec(shape, lambda i: (0,) * len(shape))
    return pl.pallas_call(
        kernel,
        grid=(nodes // tile,),
        in_specs=[
            pl.BlockSpec((tile // group, group * fanout), lambda i: (i, 0)),
            whole(nodes // 128, 128),
            whole(nodes, width),
            whole(peers * block, width),
            whole(width, width),
            whole(width, width),
            whole(1, width),
        ],
        out_specs=pl.BlockSpec((tile, width), lambda i: (i, 0)),
        out_shape=jax.ShapeDtypeStruct((nodes, width), BF16),
        scratch_shapes=[
            pltpu.VMEM((highs * LO, 2 * width), F8),
            pltpu.VMEM((tile, highs * LO), F8),
            pltpu.VMEM((hub_space, width), F32),
        ],
        compiler_params=pltpu.CompilerParams(vmem_limit_bytes=VMEM_BYTES),
        name="sage_layer",
    )(index, degree.reshape(nodes // 128, 128), features, halo, w_self, w_neigh, bias.reshape(1, width))


def solution(mesh):
    in_specs = (
        P(("groups", "node"), None),
        P(("groups", "node"), None),
        P(("groups", "node")),
        P(("groups", "node"), None, None),
        P(("groups", "node"), None),
        P(),
        P(),
        P(),
    )
    out_specs = P(("groups", "node"), None)
    return jax.shard_map(local, mesh=mesh, in_specs=in_specs, out_specs=out_specs, check_vma=False)
```

```python
import functools

import jax
import jax.numpy as jnp
from jax import lax
from jax.experimental import pallas as pl
from jax.experimental.pallas import tpu as pltpu
from jax.sharding import PartitionSpec as P

F8 = jnp.float8_e4m3fn
BF16 = jnp.bfloat16
F32 = jnp.float32
LO = 256
VMEM_BYTES = 56 * 2**20


def outgoing_kernel(send_ref, hub_ref, feat_ref, out_ref, wide, picked, *, peers, rows, hubs):
    nodes = feat_ref.shape[0]
    block = rows + hubs

    @pl.loop(0, nodes // 256)
    def _(step):
        at = pl.ds(pl.multiple_of(step * 256, 256), 256)
        wide[at, :] = feat_ref[at, :].astype(F32)

    mine = jnp.concatenate([wide[pl.ds(hub_ref[j], 1), :] for j in range(hubs)], axis=0)

    @pl.loop(0, peers)
    def _(peer):
        to = picked.at[pl.ds(pl.multiple_of(peer * block, 8), block)]
        for c in range(rows):
            to[c : c + 1, :] = wide[pl.ds(send_ref[peer * rows + c], 1), :]
        to[rows:, :] = mine

    out_ref[...] = picked[...].astype(BF16)


def split(values):
    scaled = values.astype(F32) * 64.0
    high = scaled.astype(F8)
    low = ((scaled - high.astype(F32)) * 16.0).astype(F8)
    return jnp.concatenate([high, low], axis=1)


def joined(total):
    width = total.shape[1] // 2
    return total[:, :width] * (1.0 / 64.0) + total[:, width:] * (1.0 / 1024.0)


def count_group(row, group, first, last):
    lanes = row.shape[1]
    per = lanes // group
    high = lax.shift_right_arithmetic(row, 8)
    low = row & (LO - 1)
    shape = (2 * group, lanes)
    lane_node = lax.broadcasted_iota(jnp.int32, shape, 1) // per
    sub = lax.broadcasted_iota(jnp.int32, shape, 0)
    mine = jnp.where(lane_node == sub % group, jnp.broadcast_to(high, shape) - sub // group, -100).astype(jnp.int8)
    one = jnp.ones(shape, F8)
    zero = jnp.zeros(shape, F8)
    left = jnp.concatenate([jnp.where(mine == jnp.int8(j), one, zero) for j in range(first, last, 2)], axis=0)
    lows = jnp.broadcast_to(low - 128, shape).astype(jnp.int8)
    right = jnp.concatenate(
        [jnp.where(lows == (sub + (j - 128)).astype(jnp.int8), one, zero) for j in range(0, LO, 2 * group)], axis=0
    )
    counts = lax.dot_general(left, right, (((1,), (1,)), ((), ())), preferred_element_type=F32)
    return counts.reshape(last - first, group, LO)


def fill_counts(counts, index_ref, base, tile, group, first, last, unroll):
    def pair(i, carry):
        both = [count_group(index_ref[pl.ds(base + 2 * i + j, 1), :], group, first, last) for j in range(2)]
        both = jnp.concatenate(both, axis=1).astype(F8)
        at = pl.ds(pl.multiple_of(i * 2 * group, 2 * group), 2 * group)
        for h in range(last - first):
            counts[at, h * LO : (h + 1) * LO] = both[h]
        return carry

    lax.fori_loop(0, tile // (2 * group), pair, 0, unroll=unroll)


def own_kernel(slot_ref, degree_ref, feat_ref, index_ref, table_ref, part_ref, counts, *, tile, early, group, fanout, own):
    nodes, width = feat_ref.shape
    lanes = group * fanout
    half = nodes // 128 * 8

    pick = lax.broadcasted_iota(jnp.int32, (fanout, lanes), 0) == lax.broadcasted_iota(jnp.int32, (fanout, lanes), 1) % fanout
    pick = jnp.where(pick, 1.0, 0.0).astype(BF16)
    slot = lax.broadcasted_iota(jnp.int32, (fanout, 128), 0)
    sub = lax.broadcasted_iota(jnp.int32, (128, lanes), 0)
    keep = sub % group == lax.broadcasted_iota(jnp.int32, (128, lanes), 1) // fanout

    def relay(i, carry):
        at = pl.multiple_of(i * 8, 8)
        lines = jnp.concatenate([slot_ref[pl.ds(at + half * j, 8), :] for j in range(fanout // 8)], axis=0)
        lines = jnp.where(slot < degree_ref[pl.ds(i, 1), :], lines, -1)
        high = lax.shift_right_arithmetic(lines, 8).astype(F32).astype(BF16)
        low = (lines & 255).astype(F32).astype(BF16)
        turned = [
            lax.dot_general(part, pick, (((0,), (0,)), ((), ())), preferred_element_type=F32) for part in (high, low)
        ]
        turned = jnp.where(keep, turned[0] * 256.0 + turned[1], 0.0)
        rows = [jnp.sum(turned[g * group : (g + 1) * group], axis=0, keepdims=True) for g in range(128 // group)]
        index_ref[pl.ds(pl.multiple_of(i * (128 // group), 128 // group), 128 // group), :] = jnp.concatenate(rows, axis=0).astype(
            jnp.int32
        )
        return carry

    lax.fori_loop(0, nodes // 128, relay, 0, unroll=2)

    @pl.loop(0, nodes // 256)
    def _(i):
        at = pl.ds(pl.multiple_of(i * 256, 256), 256)
        table_ref[at, :] = split(feat_ref[at, :])

    @pl.loop(0, early // tile)
    def _(t):
        fill_counts(counts, index_ref, t * (tile // group), tile, group, 0, own, 8)
        total = jnp.dot(counts[...], table_ref[...], preferred_element_type=F32)
        part_ref[pl.ds(pl.multiple_of(t * tile, tile), tile), :] = joined(total)


def layer_kernel(
    index_ref, degree_ref, part_ref, feat_ref, halo_ref, table_ref, self_ref, neigh_ref, bias_ref, out_ref,
    table, counts, wide, hub_rows, sem, *, tile, early, group, peers, rows, hubs, own, highs
):
    nodes, width = table_ref.shape[0], feat_ref.shape[1]
    step = pl.program_id(0)
    block = rows + hubs

    @pl.when(step == 0)
    def _():
        copy = pltpu.make_async_copy(table_ref, table.at[pl.ds(0, nodes)], sem)
        copy.start()
        wide[...] = halo_ref[...].astype(F32)
        hub_rows[...] = jnp.zeros_like(hub_rows)

        @pl.loop(0, peers)
        def _(i):
            at = pl.multiple_of(i * block, 8)
            table[pl.ds(pl.multiple_of(nodes + i * rows, 32), rows), :] = split(wide[pl.ds(at, rows), :])
            hub_rows[pl.ds(pl.multiple_of(i * hubs, 8), hubs), :] = wide[pl.ds(at + rows, hubs), :]

        table[nodes + peers * rows :, :] = split(hub_rows[...])
        copy.wait()

    def finish(total):
        eye = lax.broadcasted_iota(jnp.int32, (128, 128), 0) == lax.broadcasted_iota(jnp.int32, (128, 128), 1)
        ones = jnp.ones((128, width), BF16)
        spread = []
        for j in range(tile // 128):
            line = degree_ref[pl.ds(step * (tile // 128) + j, 1), :].astype(F32)
            spread.append(jnp.dot(jnp.where(eye, line, 0.0).astype(BF16), ones, preferred_element_type=F32))
        aggregate = (total / jnp.concatenate(spread, axis=0)).astype(BF16)
        mixed = jnp.dot(feat_ref[...], self_ref[...], preferred_element_type=F32)
        mixed = mixed + jnp.dot(aggregate, neigh_ref[...], preferred_element_type=F32) + bias_ref[...]
        out_ref[...] = jnp.maximum(mixed, 0.0).astype(BF16)

    @pl.when(step < early // tile)
    def _():
        fill_counts(counts, index_ref, 0, tile, group, own, highs, 8)
        total = jnp.dot(counts[:, : (highs - own) * LO], table[own * LO :, :], preferred_element_type=F32)
        finish(joined(total) + part_ref[...])

    @pl.when(step >= early // tile)
    def _():
        fill_counts(counts, index_ref, 0, tile, group, 0, highs, 8)
        finish(joined(jnp.dot(counts[...], table[...], preferred_element_type=F32)))


def local(features, neighbors, degree, send_list, hub_rows, w_self, w_neigh, bias):
    nodes, width = features.shape
    fanout = neighbors.shape[1]
    _, peers, rows = send_list.shape
    hubs = hub_rows.shape[1]
    block = rows + hubs
    group = 256 // fanout
    own = nodes // LO
    highs = -(-(nodes + peers * block) // (2 * LO)) * 2
    hub_space = highs * LO - nodes - peers * rows
    tile = 512
    early = 2048
    smem = pl.BlockSpec(memory_space=pltpu.SMEM)
    vmem = pl.BlockSpec(memory_space=pltpu.VMEM)
    params = pltpu.CompilerParams(vmem_limit_bytes=VMEM_BYTES)

    outgoing = pl.pallas_call(
        functools.partial(outgoing_kernel, peers=peers, rows=rows, hubs=hubs),
        in_specs=[smem, smem, vmem],
        out_specs=vmem,
        out_shape=jax.ShapeDtypeStruct((peers * block, width), BF16),
        scratch_shapes=[pltpu.VMEM((nodes, width), F32), pltpu.VMEM((peers * block, width), F32)],
        compiler_params=params,
        name="outgoing_rows",
    )(send_list.reshape(-1), hub_rows.reshape(-1), features)
    halo = lax.all_to_all(outgoing.reshape(peers, block, width), "node", split_axis=0, concat_axis=0, tiled=True)
    halo = halo.reshape(peers * block, width)

    lines = neighbors.T.reshape(fanout // 8, 8, nodes // 128, 128).transpose(0, 2, 1, 3).reshape(-1, 128)
    counts_of = degree.reshape(nodes // 128, 128)
    index, table, part = pl.pallas_call(
        functools.partial(own_kernel, tile=tile, early=early, group=group, fanout=fanout, own=own),
        in_specs=[vmem, vmem, vmem],
        out_specs=[vmem, vmem, vmem],
        out_shape=[
            jax.ShapeDtypeStruct((nodes // group, group * fanout), jnp.int32),
            jax.ShapeDtypeStruct((nodes, 2 * width), F8),
            jax.ShapeDtypeStruct((early, width), F32),
        ],
        scratch_shapes=[pltpu.VMEM((tile, own * LO), F8)],
        compiler_params=params,
        cost_estimate=pl.CostEstimate(flops=30_000_000_000, bytes_accessed=6_000_000, transcendentals=0),
        name="own_part",
    )(lines, counts_of, features)

    whole = lambda *shape: pl.BlockSpec(shape, lambda i: (0,) * len(shape))
    last_early = early // tile - 1
    return pl.pallas_call(
        functools.partial(
            layer_kernel, tile=tile, early=early, group=group, peers=peers, rows=rows, hubs=hubs, own=own, highs=highs
        ),
        grid=(nodes // tile,),
        in_specs=[
            pl.BlockSpec((tile // group, group * fanout), lambda i: (i, 0)),
            whole(nodes // 128, 128),
            pl.BlockSpec((tile, width), lambda i: (jnp.minimum(i, last_early), 0)),
            pl.BlockSpec((tile, width), lambda i: (i, 0)),
            whole(peers * block, width),
            pl.BlockSpec(memory_space=pl.ANY),
            whole(width, width),
            whole(width, width),
            whole(1, width),
        ],
        out_specs=pl.BlockSpec((tile, width), lambda i: (i, 0)),
        out_shape=jax.ShapeDtypeStruct((nodes, width), BF16),
        scratch_shapes=[
            pltpu.VMEM((highs * LO, 2 * width), F8),
            pltpu.VMEM((tile, highs * LO), F8),
            pltpu.VMEM((peers * block, width), F32),
            pltpu.VMEM((hub_space, width), F32),
            pltpu.SemaphoreType.DMA,
        ],
        compiler_params=params,
        name="sage_layer",
    )(index, counts_of, part, features, halo, table, w_self, w_neigh, bias.reshape(1, width))


def solution(mesh):
    in_specs = (
        P(("groups", "node"), None),
        P(("groups", "node"), None),
        P(("groups", "node")),
        P(("groups", "node"), None, None),
        P(("groups", "node"), None),
        P(),
        P(),
        P(),
    )
    out_specs = P(("groups", "node"), None)
    return jax.shard_map(local, mesh=mesh, in_specs=in_specs, out_specs=out_specs, check_vma=False)
```

```python
import functools

import jax
import jax.numpy as jnp
from jax import lax
from jax.experimental import pallas as pl
from jax.experimental.pallas import tpu as pltpu
from jax.sharding import PartitionSpec as P

F8 = jnp.float8_e4m3fn
BF16 = jnp.bfloat16
F32 = jnp.float32
LO = 256
VMEM_BYTES = 56 * 2**20
TILE = 1024
EARLY = 2048
UNROLL = 16


def outgoing_kernel(send_ref, hub_ref, feat_ref, out_ref, wide, picked, *, peers, rows, hubs):
    nodes = feat_ref.shape[0]
    block = rows + hubs

    @pl.loop(0, nodes // 512)
    def _(step):
        at = pl.ds(pl.multiple_of(step * 512, 512), 512)
        wide[at, :] = feat_ref[at, :].astype(F32)

    mine = jnp.concatenate([wide[pl.ds(hub_ref[j], 1), :] for j in range(hubs)], axis=0)

    @pl.loop(0, peers)
    def _(peer):
        to = picked.at[pl.ds(pl.multiple_of(peer * block, 8), block)]
        for c in range(rows):
            to[c : c + 1, :] = wide[pl.ds(send_ref[peer * rows + c], 1), :]
        to[rows:, :] = mine

    out_ref[...] = picked[...].astype(BF16)


def split(values):
    scaled = values.astype(F32) * 64.0
    high = scaled.astype(F8)
    low = ((scaled - high.astype(F32)) * 16.0).astype(F8)
    return jnp.concatenate([high, low], axis=1)


def joined(total):
    width = total.shape[1] // 2
    return total[:, :width] * (1.0 / 64.0) + total[:, width:] * (1.0 / 1024.0)


def count_group(row, group, first, last):
    lanes = row.shape[1]
    high = lax.shift_right_arithmetic(row, 8)
    low = row & (LO - 1)
    shape = (2 * group, lanes)
    lane_node = lax.broadcasted_iota(jnp.int32, shape, 1) % group
    sub = lax.broadcasted_iota(jnp.int32, shape, 0)
    mine = jnp.where(lane_node == sub % group, jnp.broadcast_to(high, shape) - sub // group, -100).astype(jnp.int8)
    one = jnp.ones(shape, F8)
    zero = jnp.zeros(shape, F8)
    left = jnp.concatenate([jnp.where(mine == jnp.int8(j), one, zero) for j in range(first, last, 2)], axis=0)
    lows = jnp.broadcast_to(low - 128, shape).astype(jnp.int8)
    right = jnp.concatenate(
        [jnp.where(lows == (sub + (j - 128)).astype(jnp.int8), one, zero) for j in range(0, LO, 2 * group)], axis=0
    )
    counts = lax.dot_general(left, right, (((1,), (1,)), ((), ())), preferred_element_type=F32)
    return counts.reshape(last - first, group, LO)


def group_rows(slot_ref, degree_ref, at, line, group):
    lane_slot = lax.broadcasted_iota(jnp.int32, (8, 128), 1) // group
    slot = lax.broadcasted_iota(jnp.int32, (8, 128), 0)
    parts = []
    for j in range(slot_ref.shape[0]):
        lines = jnp.where(slot + 8 * j < degree_ref[pl.ds(line, 1), :], slot_ref[j, at], -1)
        lines = pltpu.roll(lines, group, 1, stride=group, stride_axis=0)
        turned = jnp.zeros((8, 128), jnp.int32)
        for s in range(8):
            one = jnp.broadcast_to(lines[s : s + 1], (8, 128))
            turned = jnp.where(lane_slot == s, pltpu.roll(one, 0, 1, stride=group, stride_axis=0), turned)
        parts.append(turned)
    return jnp.concatenate(parts, axis=1)


def fill_counts(counts, index_ref, base, tile, group, first, last):
    def pair(i, carry):
        both = [count_group(index_ref[pl.ds(base + ((2 * i + j) ^ 7), 1), :], group, first, last) for j in range(2)]
        both = jnp.concatenate(both, axis=1).astype(F8)
        at = pl.ds(pl.multiple_of(i * 2 * group, 2 * group), 2 * group)
        for h in range(last - first):
            counts[at, h * LO : (h + 1) * LO] = both[h]
        return carry

    lax.fori_loop(0, tile // (2 * group), pair, 0, unroll=UNROLL)


def own_kernel(
    slot_ref, degree_ref, feat_ref, index_ref, table_ref, part_ref, counts, feat, table, index, sems, *, tile, early, group, own
):
    nodes = feat.shape[0]
    fetch = pltpu.make_async_copy(feat_ref, feat, sems.at[0])
    save_table = pltpu.make_async_copy(table, table_ref, sems.at[1])
    save_index = pltpu.make_async_copy(index, index_ref, sems.at[2])
    fetch.start()

    def relay(i, carry):
        index[pl.ds(pl.multiple_of(i * 8, 8), 8), :] = group_rows(slot_ref, degree_ref, i, i, group)
        return carry

    lax.fori_loop(0, nodes // 128, relay, 0, unroll=8)
    save_index.start()
    fetch.wait()

    @pl.loop(0, nodes // 512)
    def _(i):
        at = pl.ds(pl.multiple_of(i * 512, 512), 512)
        table[at, :] = split(feat[at, :])

    save_table.start()

    @pl.loop(0, early // tile)
    def _(t):
        fill_counts(counts, index, t * (tile // group), tile, group, 0, own)
        total = jnp.dot(counts[...], table[...], preferred_element_type=F32)
        part_ref[pl.ds(pl.multiple_of(t * tile, tile), tile), :] = joined(total)

    save_index.wait()
    save_table.wait()


def layer_kernel(
    index_ref, degree_ref, part_ref, feat_ref, halo_ref, table_ref, self_ref, neigh_ref, bias_ref, out_ref,
    table, counts, wide, hub_rows, sem, *, tile, early, group, peers, rows, hubs, own, highs
):
    nodes, width = table_ref.shape[0], feat_ref.shape[1]
    step = pl.program_id(0)
    block = rows + hubs
    copy = pltpu.make_async_copy(table_ref, table.at[pl.ds(0, nodes)], sem)

    @pl.when(step == 0)
    def _():
        copy.start()
        wide[...] = halo_ref[...].astype(F32)
        hub_rows[...] = jnp.zeros_like(hub_rows)

        @pl.loop(0, peers)
        def _(i):
            at = pl.multiple_of(i * block, 8)
            table[pl.ds(pl.multiple_of(nodes + i * rows, 32), rows), :] = split(wide[pl.ds(at, rows), :])
            hub_rows[pl.ds(pl.multiple_of(i * hubs, 8), hubs), :] = wide[pl.ds(at + rows, hubs), :]

        table[nodes + peers * rows :, :] = split(hub_rows[...])

    def finish(total):
        eye = lax.broadcasted_iota(jnp.int32, (128, 128), 0) == lax.broadcasted_iota(jnp.int32, (128, 128), 1)
        ones = jnp.ones((128, width), BF16)
        spread = []
        for j in range(tile // 128):
            line = degree_ref[pl.ds(step * (tile // 128) + j, 1), :].astype(F32)
            spread.append(jnp.dot(jnp.where(eye, line, 0.0).astype(BF16), ones, preferred_element_type=F32))
        aggregate = (total / jnp.concatenate(spread, axis=0)).astype(BF16)
        mixed = jnp.dot(feat_ref[...], self_ref[...], preferred_element_type=F32)
        mixed = mixed + jnp.dot(aggregate, neigh_ref[...], preferred_element_type=F32) + bias_ref[...]
        out_ref[...] = jnp.maximum(mixed, 0.0).astype(BF16)

    @pl.when(step < early // tile)
    def _():
        fill_counts(counts, index_ref, 0, tile, group, own, highs)
        total = jnp.dot(counts[:, : (highs - own) * LO], table[own * LO :, :], preferred_element_type=F32)
        finish(joined(total) + part_ref[...])

    @pl.when(step == early // tile)
    def _():
        copy.wait()

    @pl.when(step >= early // tile)
    def _():
        fill_counts(counts, index_ref, 0, tile, group, 0, highs)
        finish(joined(jnp.dot(counts[...], table[...], preferred_element_type=F32)))


def local(features, neighbors, degree, send_list, hub_rows, w_self, w_neigh, bias):
    nodes, width = features.shape
    fanout = neighbors.shape[1]
    _, peers, rows = send_list.shape
    hubs = hub_rows.shape[1]
    block = rows + hubs
    group = 256 // fanout
    own = nodes // LO
    highs = -(-(nodes + peers * block) // (2 * LO)) * 2
    hub_space = highs * LO - nodes - peers * rows
    tile = TILE
    early = EARLY
    smem = pl.BlockSpec(memory_space=pltpu.SMEM)
    vmem = pl.BlockSpec(memory_space=pltpu.VMEM)
    params = pltpu.CompilerParams(vmem_limit_bytes=VMEM_BYTES)

    lines = neighbors.T.reshape(fanout // 8, 8, nodes // 128, 128).transpose(0, 2, 1, 3)
    degrees = degree.reshape(nodes // 128, 128)
    outgoing = pl.pallas_call(
        functools.partial(outgoing_kernel, peers=peers, rows=rows, hubs=hubs),
        in_specs=[smem, smem, vmem],
        out_specs=vmem,
        out_shape=jax.ShapeDtypeStruct((peers * block, width), BF16),
        scratch_shapes=[pltpu.VMEM((nodes, width), F32), pltpu.VMEM((peers * block, width), F32)],
        compiler_params=params,
        name="outgoing_rows",
    )(send_list.reshape(-1), hub_rows.reshape(-1), features)
    halo = lax.all_to_all(outgoing.reshape(peers, block, width), "node", split_axis=0, concat_axis=0, tiled=True)
    halo = halo.reshape(peers * block, width)

    index, table, part = pl.pallas_call(
        functools.partial(own_kernel, tile=tile, early=early, group=group, own=own),
        grid=(1,),
        in_specs=[
            pl.BlockSpec((fanout // 8, nodes // 128, 8, 128), lambda i: (0, 0, 0, 0)),
            pl.BlockSpec((nodes // 128, 128), lambda i: (0, 0)),
            pl.BlockSpec(memory_space=pl.ANY),
        ],
        out_specs=[
            pl.BlockSpec(memory_space=pl.ANY),
            pl.BlockSpec(memory_space=pl.ANY),
            pl.BlockSpec((early, width), lambda i: (0, 0)),
        ],
        out_shape=[
            jax.ShapeDtypeStruct((nodes // group, group * fanout), jnp.int32),
            jax.ShapeDtypeStruct((nodes, 2 * width), F8),
            jax.ShapeDtypeStruct((early, width), F32),
        ],
        scratch_shapes=[
            pltpu.VMEM((tile, own * LO), F8),
            pltpu.VMEM((nodes, width), BF16),
            pltpu.VMEM((nodes, 2 * width), F8),
            pltpu.VMEM((nodes // group, group * fanout), jnp.int32),
            pltpu.SemaphoreType.DMA((3,)),
        ],
        compiler_params=params,
        cost_estimate=pl.CostEstimate(flops=30_000_000_000, bytes_accessed=6_000_000, transcendentals=0),
        name="own_part",
    )(lines, degrees, features)

    whole = lambda *shape: pl.BlockSpec(shape, lambda i: (0,) * len(shape))
    last_early = early // tile - 1
    return pl.pallas_call(
        functools.partial(
            layer_kernel, tile=tile, early=early, group=group, peers=peers, rows=rows, hubs=hubs, own=own, highs=highs
        ),
        grid=(nodes // tile,),
        in_specs=[
            pl.BlockSpec((tile // group, group * fanout), lambda i: (i, 0)),
            whole(nodes // 128, 128),
            pl.BlockSpec((tile, width), lambda i: (jnp.minimum(i, last_early), 0)),
            pl.BlockSpec((tile, width), lambda i: (i, 0)),
            whole(peers * block, width),
            pl.BlockSpec(memory_space=pl.ANY),
            whole(width, width),
            whole(width, width),
            whole(1, width),
        ],
        out_specs=pl.BlockSpec((tile, width), lambda i: (i, 0)),
        out_shape=jax.ShapeDtypeStruct((nodes, width), BF16),
        scratch_shapes=[
            pltpu.VMEM((highs * LO, 2 * width), F8),
            pltpu.VMEM((tile, highs * LO), F8),
            pltpu.VMEM((peers * block, width), F32),
            pltpu.VMEM((hub_space, width), F32),
            pltpu.SemaphoreType.DMA,
        ],
        compiler_params=params,
        name="sage_layer",
    )(index, degrees, part, features, halo, table, w_self, w_neigh, bias.reshape(1, width))


def solution(mesh):
    in_specs = (
        P(("groups", "node"), None),
        P(("groups", "node"), None),
        P(("groups", "node")),
        P(("groups", "node"), None, None),
        P(("groups", "node"), None),
        P(),
        P(),
        P(),
    )
    out_specs = P(("groups", "node"), None)
    return jax.shard_map(local, mesh=mesh, in_specs=in_specs, out_specs=out_specs, check_vma=False)
```

```python
import functools

import jax
import jax.numpy as jnp
from jax import lax
from jax.experimental import pallas as pl
from jax.experimental.pallas import tpu as pltpu
from jax.sharding import PartitionSpec as P

F8 = jnp.float8_e4m3fn
BF16 = jnp.bfloat16
F32 = jnp.float32
LO = 256
VMEM_BYTES = 255 * 2**18
TILE = 1024
EARLY = 2048
UNROLL = 16


def outgoing_kernel(send_ref, hub_ref, feat_ref, out_ref, wide, picked, *, peers, rows, hubs):
    nodes = feat_ref.shape[0]
    block = rows + hubs

    @pl.loop(0, nodes // 512)
    def _(step):
        at = pl.ds(pl.multiple_of(step * 512, 512), 512)
        wide[at, :] = feat_ref[at, :].astype(F32)

    mine = jnp.concatenate([wide[pl.ds(hub_ref[j], 1), :] for j in range(hubs)], axis=0)

    def gather(peer):
        to = picked.at[pl.ds(peer * block, block)]
        for c in range(rows):
            to[c : c + 1, :] = wide[pl.ds(send_ref[peer * rows + c], 1), :]
        to[rows:, :] = mine

    if peers <= 16:
        for peer in range(peers):
            gather(peer)
    else:
        pl.loop(0, peers)(gather)

    out_ref[...] = picked[...].astype(BF16)


def split(values):
    scaled = values.astype(F32) * 64.0
    high = scaled.astype(F8)
    low = ((scaled - high.astype(F32)) * 16.0).astype(F8)
    return jnp.concatenate([high, low], axis=1)


def joined(total):
    width = total.shape[1] // 2
    return total[:, :width] * (1.0 / 64.0) + total[:, width:] * (1.0 / 1024.0)


def count_group(row, group, first, last):
    lanes = row.shape[1]
    high = lax.shift_right_arithmetic(row, 8)
    low = row & (LO - 1)
    shape = (2 * group, lanes)
    lane_node = lax.broadcasted_iota(jnp.int32, shape, 1) % group
    sub = lax.broadcasted_iota(jnp.int32, shape, 0)
    mine = jnp.where(lane_node == sub % group, jnp.broadcast_to(high, shape) - sub // group, -100).astype(jnp.int8)
    one = jnp.ones(shape, F8)
    zero = jnp.zeros(shape, F8)
    left = jnp.concatenate([jnp.where(mine == jnp.int8(j), one, zero) for j in range(first, last, 2)], axis=0)
    lows = jnp.broadcast_to(low - 128, shape).astype(jnp.int8)
    right = jnp.concatenate(
        [jnp.where(lows == (sub + (j - 128)).astype(jnp.int8), one, zero) for j in range(0, LO, 2 * group)], axis=0
    )
    counts = lax.dot_general(left, right, (((1,), (1,)), ((), ())), preferred_element_type=F32)
    return counts.reshape(last - first, group, LO)


def group_rows(slot_ref, degree_ref, at, line, group):
    lane_slot = lax.broadcasted_iota(jnp.int32, (8, 128), 1) // group
    slot = lax.broadcasted_iota(jnp.int32, (8, 128), 0)
    parts = []
    for j in range(slot_ref.shape[0]):
        lines = jnp.where(slot + 8 * j < degree_ref[pl.ds(line, 1), :], slot_ref[j, at], -1)
        lines = pltpu.roll(lines, group, 1, stride=group, stride_axis=0)
        turned = jnp.zeros((8, 128), jnp.int32)
        for s in range(8):
            one = jnp.broadcast_to(lines[s : s + 1], (8, 128))
            turned = jnp.where(lane_slot == s, pltpu.roll(one, 0, 1, stride=group, stride_axis=0), turned)
        parts.append(turned)
    return jnp.concatenate(parts, axis=1)


def fill_counts(counts, index_ref, base, tile, group, first, last, beside=None):
    def pair(i, carry):
        both = [count_group(index_ref[pl.ds(base + ((2 * i + j) ^ 7), 1), :], group, first, last) for j in range(2)]
        both = jnp.concatenate(both, axis=1).astype(F8)
        at = pl.ds(pl.multiple_of(i * 2 * group, 2 * group), 2 * group)
        for h in range(last - first):
            counts[at, h * LO : (h + 1) * LO] = both[h]
        if beside is not None:
            beside(i)
        return carry

    lax.fori_loop(0, tile // (2 * group), pair, 0, unroll=UNROLL)


def own_kernel(
    slot_ref, degree_ref, feat_ref, index_ref, table_ref, part_ref,
    counts, feat, table, index, later, sems, *, tile, early, group, own
):
    nodes = feat.shape[0]
    lines = nodes // 128
    early_lines = early // 128
    last = early // tile - 1
    fetch = pltpu.make_async_copy(feat_ref, feat, sems.at[0])
    save_table = pltpu.make_async_copy(table, table_ref, sems.at[1])
    save_index = pltpu.make_async_copy(index, index_ref.at[pl.ds(0, early // group)], sems.at[2])
    save_later = pltpu.make_async_copy(later, index_ref.at[pl.ds(early // group, (nodes - early) // group)], sems.at[3])
    fetch.start()

    def relay(i, carry):
        index[pl.ds(pl.multiple_of(i * 8, 8), 8), :] = group_rows(slot_ref, degree_ref, i, i, group)
        return carry

    lax.fori_loop(0, early_lines, relay, 0, unroll=8)
    save_index.start()
    fetch.wait()

    @pl.loop(0, nodes // 512)
    def _(i):
        at = pl.ds(pl.multiple_of(i * 512, 512), 512)
        table[at, :] = split(feat[at, :])

    save_table.start()

    @pl.loop(0, last + 1)
    def _(t):
        def relay_later(i):
            line = jnp.minimum(t * (tile // (2 * group)) + i, lines - early_lines - 1)
            rows = group_rows(slot_ref, degree_ref, early_lines + line, early_lines + line, group)
            later[pl.ds(pl.multiple_of(line * 8, 8), 8), :] = rows

        fill_counts(counts, index, t * (tile // group), tile, group, 0, own, relay_later)

        @pl.when(t == last)
        def _():
            save_later.start()

        total = jnp.dot(counts[...], table[...], preferred_element_type=F32)
        part_ref[pl.ds(pl.multiple_of(t * tile, tile), tile), :] = joined(total)

    save_index.wait()
    save_table.wait()
    save_later.wait()


def layer_kernel(
    index_ref, degree_ref, part_ref, feat_ref, halo_ref, table_ref, self_ref, neigh_ref, bias_ref, out_ref,
    table, counts, halo, wide, hub_rows, sems, *, tile, early, group, peers, rows, hubs, own, highs
):
    nodes, width = table_ref.shape[0], feat_ref.shape[1]
    step = pl.program_id(0)
    block = rows + hubs
    own_copy = pltpu.make_async_copy(table_ref, table.at[pl.ds(0, nodes)], sems.at[0])
    halo_copy = pltpu.make_async_copy(halo_ref, halo, sems.at[1])

    @pl.when(step == 0)
    def _():
        halo_copy.start()
        own_copy.start()

    def add_halo():
        halo_copy.wait()
        wide[...] = halo[...].astype(F32)
        hub_rows[...] = jnp.zeros_like(hub_rows)

        @pl.loop(0, peers, unroll=4)
        def _(i):
            at = pl.multiple_of(i * block, 8)
            table[pl.ds(pl.multiple_of(nodes + i * rows, 32), rows), :] = split(wide[pl.ds(at, rows), :])
            hub_rows[pl.ds(pl.multiple_of(i * hubs, 8), hubs), :] = wide[pl.ds(at + rows, hubs), :]

        table[nodes + peers * rows :, :] = split(hub_rows[...])

    def finish(total):
        eye = lax.broadcasted_iota(jnp.int32, (128, 128), 0) == lax.broadcasted_iota(jnp.int32, (128, 128), 1)
        ones = jnp.ones((128, width), BF16)
        spread = []
        for j in range(tile // 128):
            line = degree_ref[pl.ds(step * (tile // 128) + j, 1), :].astype(F32)
            spread.append(jnp.dot(jnp.where(eye, line, 0.0).astype(BF16), ones, preferred_element_type=F32))
        aggregate = (total / jnp.concatenate(spread, axis=0)).astype(BF16)
        mixed = jnp.dot(feat_ref[...], self_ref[...], preferred_element_type=F32)
        mixed = mixed + jnp.dot(aggregate, neigh_ref[...], preferred_element_type=F32) + bias_ref[...]
        out_ref[...] = jnp.maximum(mixed, 0.0).astype(BF16)

    @pl.when(step < early // tile)
    def _():
        fill_counts(counts, index_ref, 0, tile, group, own, highs)
        pl.when(step == 0)(add_halo)
        total = jnp.dot(counts[:, : (highs - own) * LO], table[own * LO :, :], preferred_element_type=F32)
        finish(joined(total) + part_ref[...])

    @pl.when(step == early // tile)
    def _():
        own_copy.wait()

    @pl.when(step >= early // tile)
    def _():
        fill_counts(counts, index_ref, 0, tile, group, 0, highs)
        finish(joined(jnp.dot(counts[...], table[...], preferred_element_type=F32)))


def local(features, neighbors, degree, send_list, hub_rows, w_self, w_neigh, bias):
    nodes, width = features.shape
    fanout = neighbors.shape[1]
    _, peers, rows = send_list.shape
    hubs = hub_rows.shape[1]
    block = rows + hubs
    group = 256 // fanout
    own = nodes // LO
    highs = -(-(nodes + peers * block) // (2 * LO)) * 2
    hub_space = highs * LO - nodes - peers * rows
    tile = TILE
    early = EARLY
    smem = pl.BlockSpec(memory_space=pltpu.SMEM)
    vmem = pl.BlockSpec(memory_space=pltpu.VMEM)
    params = pltpu.CompilerParams(vmem_limit_bytes=VMEM_BYTES)

    lines = neighbors.T.reshape(fanout // 8, 8, nodes // 128, 128).transpose(0, 2, 1, 3)
    degrees = degree.reshape(nodes // 128, 128)
    outgoing = pl.pallas_call(
        functools.partial(outgoing_kernel, peers=peers, rows=rows, hubs=hubs),
        in_specs=[smem, smem, vmem],
        out_specs=vmem,
        out_shape=jax.ShapeDtypeStruct((peers * block, width), BF16),
        scratch_shapes=[pltpu.VMEM((nodes, width), F32), pltpu.VMEM((peers * block, width), F32)],
        compiler_params=params,
        name="outgoing_rows",
    )(send_list.reshape(-1), hub_rows.reshape(-1), features)
    halo = lax.all_to_all(outgoing.reshape(peers, block, width), "node", split_axis=0, concat_axis=0, tiled=True)
    halo = halo.reshape(peers * block, width)

    index, table, part = pl.pallas_call(
        functools.partial(own_kernel, tile=tile, early=early, group=group, own=own),
        grid=(1,),
        in_specs=[
            pl.BlockSpec((fanout // 8, nodes // 128, 8, 128), lambda i: (0, 0, 0, 0)),
            pl.BlockSpec((nodes // 128, 128), lambda i: (0, 0)),
            pl.BlockSpec(memory_space=pl.ANY),
        ],
        out_specs=[
            pl.BlockSpec(memory_space=pl.ANY),
            pl.BlockSpec(memory_space=pl.ANY),
            pl.BlockSpec((early, width), lambda i: (0, 0)),
        ],
        out_shape=[
            jax.ShapeDtypeStruct((nodes // group, group * fanout), jnp.int32),
            jax.ShapeDtypeStruct((nodes, 2 * width), F8),
            jax.ShapeDtypeStruct((early, width), F32),
        ],
        scratch_shapes=[
            pltpu.VMEM((tile, own * LO), F8),
            pltpu.VMEM((nodes, width), BF16),
            pltpu.VMEM((nodes, 2 * width), F8),
            pltpu.VMEM((early // group, group * fanout), jnp.int32),
            pltpu.VMEM(((nodes - early) // group, group * fanout), jnp.int32),
            pltpu.SemaphoreType.DMA((4,)),
        ],
        compiler_params=params,
        cost_estimate=pl.CostEstimate(flops=30_000_000_000, bytes_accessed=6_000_000, transcendentals=0),
        name="own_part",
    )(lines, degrees, features)

    whole = lambda *shape: pl.BlockSpec(shape, lambda i: (0,) * len(shape))
    last_early = early // tile - 1
    return pl.pallas_call(
        functools.partial(
            layer_kernel, tile=tile, early=early, group=group, peers=peers, rows=rows, hubs=hubs, own=own, highs=highs
        ),
        grid=(nodes // tile,),
        in_specs=[
            pl.BlockSpec((tile // group, group * fanout), lambda i: (i, 0)),
            whole(nodes // 128, 128),
            pl.BlockSpec((tile, width), lambda i: (jnp.minimum(i, last_early), 0)),
            pl.BlockSpec((tile, width), lambda i: (i, 0)),
            pl.BlockSpec(memory_space=pl.ANY),
            pl.BlockSpec(memory_space=pl.ANY),
            whole(width, width),
            whole(width, width),
            whole(1, width),
        ],
        out_specs=pl.BlockSpec((tile, width), lambda i: (i, 0)),
        out_shape=jax.ShapeDtypeStruct((nodes, width), BF16),
        scratch_shapes=[
            pltpu.VMEM((highs * LO, 2 * width), F8),
            pltpu.VMEM((tile, highs * LO), F8),
            pltpu.VMEM((peers * block, width), BF16),
            pltpu.VMEM((peers * block, width), F32),
            pltpu.VMEM((hub_space, width), F32),
            pltpu.SemaphoreType.DMA((2,)),
        ],
        compiler_params=params,
        name="sage_layer",
    )(index, degrees, part, features, halo, table, w_self, w_neigh, bias.reshape(1, width))


def solution(mesh):
    in_specs = (
        P(("groups", "node"), None),
        P(("groups", "node"), None),
        P(("groups", "node")),
        P(("groups", "node"), None, None),
        P(("groups", "node"), None),
        P(),
        P(),
        P(),
    )
    out_specs = P(("groups", "node"), None)
    return jax.shard_map(local, mesh=mesh, in_specs=in_specs, out_specs=out_specs, check_vma=False)
```

```python
import functools

import jax
import jax.numpy as jnp
from jax import lax
from jax.experimental import pallas as pl
from jax.experimental.pallas import tpu as pltpu
from jax.sharding import PartitionSpec as P

F8 = jnp.float8_e4m3fn
BF16 = jnp.bfloat16
F32 = jnp.float32
LO = 256
VMEM_BYTES = 255 * 2**18
TILE = 1024
EARLY = 2048
UNROLL = 16


def outgoing_kernel(send_ref, hub_ref, feat_ref, out_ref, wide, picked, *, peers, rows, hubs):
    nodes = feat_ref.shape[0]
    block = rows + hubs

    @pl.loop(0, nodes // 512)
    def _(step):
        at = pl.ds(pl.multiple_of(step * 512, 512), 512)
        wide[at, :] = feat_ref[at, :].astype(F32)

    mine = jnp.concatenate([wide[pl.ds(hub_ref[j], 1), :] for j in range(hubs)], axis=0)

    def gather(peer):
        to = picked.at[pl.ds(peer * block, block)]
        for c in range(rows):
            to[c : c + 1, :] = wide[pl.ds(send_ref[peer * rows + c], 1), :]
        to[rows:, :] = mine

    if peers <= 16:
        for peer in range(peers):
            gather(peer)
    else:
        pl.loop(0, peers)(gather)

    out_ref[...] = picked[...].astype(BF16)


def largest(values):
    return jnp.max(jnp.abs(values.astype(F32)).reshape(-1, 8, values.shape[1]), axis=0)


def fit(most):
    most = jnp.broadcast_to(jnp.max(jnp.max(most, axis=0, keepdims=True), axis=1, keepdims=True), most.shape)
    scale = jnp.ones_like(most)
    inverse = jnp.ones_like(most)
    for bits in (32, 16, 8, 4, 2, 1):
        fits = most * (scale * 2.0**bits) <= 448.0
        scale = jnp.where(fits, scale * 2.0**bits, scale)
        inverse = jnp.where(fits, inverse * 2.0**-bits, inverse)
    return scale, inverse


def split(values, scale):
    scaled = values.astype(F32) * scale
    high = scaled.astype(F8)
    low = ((scaled - high.astype(F32)) * 16.0).astype(F8)
    return jnp.concatenate([high, low], axis=1)


def joined(total, inverse):
    width = total.shape[1] // 2
    return (total[:, :width] + total[:, width:] * (1.0 / 16.0)) * inverse


def count_group(row, group, first, last):
    lanes = row.shape[1]
    high = lax.shift_right_arithmetic(row, 8)
    low = row & (LO - 1)
    shape = (2 * group, lanes)
    lane_node = lax.broadcasted_iota(jnp.int32, shape, 1) % group
    sub = lax.broadcasted_iota(jnp.int32, shape, 0)
    mine = jnp.where(lane_node == sub % group, jnp.broadcast_to(high, shape) - sub // group, -100).astype(jnp.int8)
    one = jnp.ones(shape, F8)
    zero = jnp.zeros(shape, F8)
    left = jnp.concatenate([jnp.where(mine == jnp.int8(j), one, zero) for j in range(first, last, 2)], axis=0)
    lows = jnp.broadcast_to(low - 128, shape).astype(jnp.int8)
    right = jnp.concatenate(
        [jnp.where(lows == (sub + (j - 128)).astype(jnp.int8), one, zero) for j in range(0, LO, 2 * group)], axis=0
    )
    counts = lax.dot_general(left, right, (((1,), (1,)), ((), ())), preferred_element_type=F32)
    return counts.reshape(last - first, group, LO)


def group_rows(slot_ref, degree_ref, at, line, group):
    lane_slot = lax.broadcasted_iota(jnp.int32, (8, 128), 1) // group
    slot = lax.broadcasted_iota(jnp.int32, (8, 128), 0)
    parts = []
    for j in range(slot_ref.shape[0]):
        lines = jnp.where(slot + 8 * j < degree_ref[pl.ds(line, 1), :], slot_ref[j, at], -1)
        lines = pltpu.roll(lines, group, 1, stride=group, stride_axis=0)
        turned = jnp.zeros((8, 128), jnp.int32)
        for s in range(8):
            one = jnp.broadcast_to(lines[s : s + 1], (8, 128))
            turned = jnp.where(lane_slot == s, pltpu.roll(one, 0, 1, stride=group, stride_axis=0), turned)
        parts.append(turned)
    return jnp.concatenate(parts, axis=1)


def fill_counts(counts, index_ref, base, tile, group, first, last, beside=None):
    def pair(i, carry):
        both = [count_group(index_ref[pl.ds(base + ((2 * i + j) ^ 7), 1), :], group, first, last) for j in range(2)]
        both = jnp.concatenate(both, axis=1).astype(F8)
        at = pl.ds(pl.multiple_of(i * 2 * group, 2 * group), 2 * group)
        for h in range(last - first):
            counts[at, h * LO : (h + 1) * LO] = both[h]
        if beside is not None:
            beside(i)
        return carry

    lax.fori_loop(0, tile // (2 * group), pair, 0, unroll=UNROLL)


def own_kernel(
    slot_ref, degree_ref, feat_ref, index_ref, table_ref, part_ref, inverse_ref,
    counts, feat, table, index, later, sems, *, tile, early, group, own
):
    nodes = feat.shape[0]
    lines = nodes // 128
    early_lines = early // 128
    last = early // tile - 1
    fetch = pltpu.make_async_copy(feat_ref, feat, sems.at[0])
    save_table = pltpu.make_async_copy(table, table_ref, sems.at[1])
    save_index = pltpu.make_async_copy(index, index_ref.at[pl.ds(0, early // group)], sems.at[2])
    save_later = pltpu.make_async_copy(later, index_ref.at[pl.ds(early // group, (nodes - early) // group)], sems.at[3])
    fetch.start()

    def relay(i, carry):
        index[pl.ds(pl.multiple_of(i * 8, 8), 8), :] = group_rows(slot_ref, degree_ref, i, i, group)
        return carry

    lax.fori_loop(0, early_lines, relay, 0, unroll=8)
    save_index.start()
    fetch.wait()

    def most_of(i, most):
        return jnp.maximum(most, largest(feat[pl.ds(pl.multiple_of(i * 512, 512), 512), :]))

    scale, inverse_ref[...] = fit(lax.fori_loop(0, nodes // 512, most_of, jnp.zeros(inverse_ref.shape, F32)))

    @pl.loop(0, nodes // 512)
    def _(i):
        at = pl.ds(pl.multiple_of(i * 512, 512), 512)
        table[at, :] = split(feat[at, :], scale[:1])

    save_table.start()

    @pl.loop(0, last + 1)
    def _(t):
        def relay_later(i):
            line = jnp.minimum(t * (tile // (2 * group)) + i, lines - early_lines - 1)
            rows = group_rows(slot_ref, degree_ref, early_lines + line, early_lines + line, group)
            later[pl.ds(pl.multiple_of(line * 8, 8), 8), :] = rows

        fill_counts(counts, index, t * (tile // group), tile, group, 0, own, relay_later)

        @pl.when(t == last)
        def _():
            save_later.start()

        total = jnp.dot(counts[...], table[...], preferred_element_type=F32)
        part_ref[pl.ds(pl.multiple_of(t * tile, tile), tile), :] = joined(total, inverse_ref[:1])

    save_index.wait()
    save_table.wait()
    save_later.wait()


def layer_kernel(
    index_ref, degree_ref, part_ref, own_inverse, feat_ref, halo_ref, table_ref, self_ref, neigh_ref, bias_ref, out_ref,
    table, counts, halo_inverse, halo, wide, hub_rows, sems, *, tile, early, group, peers, rows, hubs, own, highs
):
    nodes, width = table_ref.shape[0], feat_ref.shape[1]
    step = pl.program_id(0)
    block = rows + hubs
    own_copy = pltpu.make_async_copy(table_ref, table.at[pl.ds(0, nodes)], sems.at[0])
    halo_copy = pltpu.make_async_copy(halo_ref, halo, sems.at[1])

    @pl.when(step == 0)
    def _():
        halo_copy.start()
        own_copy.start()

    def add_halo():
        halo_copy.wait()
        wide[...] = halo[...].astype(F32)
        scale, halo_inverse[...] = fit(largest(wide[...]))
        hub_rows[...] = jnp.zeros_like(hub_rows)

        @pl.loop(0, peers, unroll=4)
        def _(i):
            at = pl.multiple_of(i * block, 8)
            table[pl.ds(pl.multiple_of(nodes + i * rows, 32), rows), :] = split(wide[pl.ds(at, rows), :], scale[:1])
            hub_rows[pl.ds(pl.multiple_of(i * hubs, 8), hubs), :] = wide[pl.ds(at + rows, hubs), :]

        table[nodes + peers * rows :, :] = split(hub_rows[...], scale[:1])

    def finish(total):
        eye = lax.broadcasted_iota(jnp.int32, (128, 128), 0) == lax.broadcasted_iota(jnp.int32, (128, 128), 1)
        ones = jnp.ones((128, width), BF16)
        spread = []
        for j in range(tile // 128):
            line = degree_ref[pl.ds(step * (tile // 128) + j, 1), :].astype(F32)
            spread.append(jnp.dot(jnp.where(eye, line, 0.0).astype(BF16), ones, preferred_element_type=F32))
        aggregate = (total / jnp.concatenate(spread, axis=0)).astype(BF16)
        mixed = jnp.dot(feat_ref[...], self_ref[...], preferred_element_type=F32)
        mixed = mixed + jnp.dot(aggregate, neigh_ref[...], preferred_element_type=F32) + bias_ref[...]
        out_ref[...] = jnp.maximum(mixed, 0.0).astype(BF16)

    @pl.when(step < early // tile)
    def _():
        fill_counts(counts, index_ref, 0, tile, group, own, highs)
        pl.when(step == 0)(add_halo)
        total = jnp.dot(counts[:, : (highs - own) * LO], table[own * LO :, :], preferred_element_type=F32)
        finish(joined(total, halo_inverse[:1]) + part_ref[...])

    @pl.when(step == early // tile)
    def _():
        own_copy.wait()

    @pl.when(step >= early // tile)
    def _():
        fill_counts(counts, index_ref, 0, tile, group, 0, highs)
        total = jnp.dot(counts[:, own * LO :], table[own * LO :, :], preferred_element_type=F32)
        total = joined(total, halo_inverse[:1])
        rest = jnp.dot(counts[:, : own * LO], table[: own * LO, :], preferred_element_type=F32)
        finish(total + joined(rest, own_inverse[:1]))


def local(features, neighbors, degree, send_list, hub_rows, w_self, w_neigh, bias):
    nodes, width = features.shape
    fanout = neighbors.shape[1]
    _, peers, rows = send_list.shape
    hubs = hub_rows.shape[1]
    block = rows + hubs
    group = 256 // fanout
    own = nodes // LO
    highs = -(-(nodes + peers * block) // (2 * LO)) * 2
    hub_space = highs * LO - nodes - peers * rows
    tile = TILE
    early = EARLY
    smem = pl.BlockSpec(memory_space=pltpu.SMEM)
    vmem = pl.BlockSpec(memory_space=pltpu.VMEM)
    params = pltpu.CompilerParams(vmem_limit_bytes=VMEM_BYTES)

    lines = neighbors.T.reshape(fanout // 8, 8, nodes // 128, 128).transpose(0, 2, 1, 3)
    degrees = degree.reshape(nodes // 128, 128)
    outgoing = pl.pallas_call(
        functools.partial(outgoing_kernel, peers=peers, rows=rows, hubs=hubs),
        in_specs=[smem, smem, vmem],
        out_specs=vmem,
        out_shape=jax.ShapeDtypeStruct((peers * block, width), BF16),
        scratch_shapes=[pltpu.VMEM((nodes, width), F32), pltpu.VMEM((peers * block, width), F32)],
        compiler_params=params,
        name="outgoing_rows",
    )(send_list.reshape(-1), hub_rows.reshape(-1), features)
    halo = lax.all_to_all(outgoing.reshape(peers, block, width), "node", split_axis=0, concat_axis=0, tiled=True)
    halo = halo.reshape(peers * block, width)

    index, table, part, inverse = pl.pallas_call(
        functools.partial(own_kernel, tile=tile, early=early, group=group, own=own),
        grid=(1,),
        in_specs=[
            pl.BlockSpec((fanout // 8, nodes // 128, 8, 128), lambda i: (0, 0, 0, 0)),
            pl.BlockSpec((nodes // 128, 128), lambda i: (0, 0)),
            pl.BlockSpec(memory_space=pl.ANY),
        ],
        out_specs=[
            pl.BlockSpec(memory_space=pl.ANY),
            pl.BlockSpec(memory_space=pl.ANY),
            pl.BlockSpec((early, width), lambda i: (0, 0)),
            pl.BlockSpec((8, width), lambda i: (0, 0)),
        ],
        out_shape=[
            jax.ShapeDtypeStruct((nodes // group, group * fanout), jnp.int32),
            jax.ShapeDtypeStruct((nodes, 2 * width), F8),
            jax.ShapeDtypeStruct((early, width), F32),
            jax.ShapeDtypeStruct((8, width), F32),
        ],
        scratch_shapes=[
            pltpu.VMEM((tile, own * LO), F8),
            pltpu.VMEM((nodes, width), BF16),
            pltpu.VMEM((nodes, 2 * width), F8),
            pltpu.VMEM((early // group, group * fanout), jnp.int32),
            pltpu.VMEM(((nodes - early) // group, group * fanout), jnp.int32),
            pltpu.SemaphoreType.DMA((4,)),
        ],
        compiler_params=params,
        cost_estimate=pl.CostEstimate(flops=30_000_000_000, bytes_accessed=6_000_000, transcendentals=0),
        name="own_part",
    )(lines, degrees, features)

    whole = lambda *shape: pl.BlockSpec(shape, lambda i: (0,) * len(shape))
    last_early = early // tile - 1
    return pl.pallas_call(
        functools.partial(
            layer_kernel, tile=tile, early=early, group=group, peers=peers, rows=rows, hubs=hubs, own=own, highs=highs
        ),
        grid=(nodes // tile,),
        in_specs=[
            pl.BlockSpec((tile // group, group * fanout), lambda i: (i, 0)),
            whole(nodes // 128, 128),
            pl.BlockSpec((tile, width), lambda i: (jnp.minimum(i, last_early), 0)),
            whole(8, width),
            pl.BlockSpec((tile, width), lambda i: (i, 0)),
            pl.BlockSpec(memory_space=pl.ANY),
            pl.BlockSpec(memory_space=pl.ANY),
            whole(width, width),
            whole(width, width),
            whole(1, width),
        ],
        out_specs=pl.BlockSpec((tile, width), lambda i: (i, 0)),
        out_shape=jax.ShapeDtypeStruct((nodes, width), BF16),
        scratch_shapes=[
            pltpu.VMEM((highs * LO, 2 * width), F8),
            pltpu.VMEM((tile, highs * LO), F8),
            pltpu.VMEM((8, width), F32),
            pltpu.VMEM((peers * block, width), BF16),
            pltpu.VMEM((peers * block, width), F32),
            pltpu.VMEM((hub_space, width), F32),
            pltpu.SemaphoreType.DMA((2,)),
        ],
        compiler_params=params,
        name="sage_layer",
    )(index, degrees, part, inverse, features, halo, table, w_self, w_neigh, bias.reshape(1, width))


def solution(mesh):
    in_specs = (
        P(("groups", "node"), None),
        P(("groups", "node"), None),
        P(("groups", "node")),
        P(("groups", "node"), None, None),
        P(("groups", "node"), None),
        P(),
        P(),
        P(),
    )
    out_specs = P(("groups", "node"), None)
    return jax.shard_map(local, mesh=mesh, in_specs=in_specs, out_specs=out_specs, check_vma=False)
```

```python
import functools

import jax
import jax.numpy as jnp
from jax import lax
from jax.experimental import pallas as pl
from jax.experimental.pallas import tpu as pltpu
from jax.sharding import PartitionSpec as P

F8 = jnp.float8_e4m3fn
BF16 = jnp.bfloat16
F32 = jnp.float32
LO = 256
VMEM_BYTES = 255 * 2**18
TILE = 1024
EARLY = 2048
UNROLL = 16


def outgoing_kernel(send_ref, hub_ref, feat_ref, out_ref, most_ref, wide, picked, *, peers, rows, hubs):
    nodes = feat_ref.shape[0]
    block = rows + hubs

    def widen(step, most):
        at = pl.ds(pl.multiple_of(step * 512, 512), 512)
        values = feat_ref[at, :].astype(F32)
        wide[at, :] = values
        return jnp.maximum(most, largest(values))

    most_ref[...] = lax.fori_loop(0, nodes // 512, widen, jnp.zeros(most_ref.shape, F32))

    mine = jnp.concatenate([wide[pl.ds(hub_ref[j], 1), :] for j in range(hubs)], axis=0)

    def gather(peer):
        to = picked.at[pl.ds(peer * block, block)]
        for c in range(rows):
            to[c : c + 1, :] = wide[pl.ds(send_ref[peer * rows + c], 1), :]
        to[rows:, :] = mine

    if peers <= 16:
        for peer in range(peers):
            gather(peer)
    else:
        pl.loop(0, peers)(gather)

    out_ref[...] = picked[...].astype(BF16)


def largest(values):
    return jnp.max(jnp.abs(values.astype(F32)).reshape(-1, 8, values.shape[1]), axis=0)


def fit(most):
    most = jnp.broadcast_to(jnp.max(jnp.max(most, axis=0, keepdims=True), axis=1, keepdims=True), most.shape)
    scale = jnp.ones_like(most)
    inverse = jnp.ones_like(most)
    for bits in (32, 16, 8, 4, 2, 1):
        fits = most * (scale * 2.0**bits) <= 448.0
        scale = jnp.where(fits, scale * 2.0**bits, scale)
        inverse = jnp.where(fits, inverse * 2.0**-bits, inverse)
    return scale, inverse


def split(values, scale):
    scaled = values.astype(F32) * scale
    high = scaled.astype(F8)
    low = ((scaled - high.astype(F32)) * 16.0).astype(F8)
    return jnp.concatenate([high, low], axis=1)


def joined(total, inverse):
    width = total.shape[1] // 2
    return (total[:, :width] + total[:, width:] * (1.0 / 16.0)) * inverse


def count_group(row, group, first, last):
    lanes = row.shape[1]
    high = lax.shift_right_arithmetic(row, 8)
    low = row & (LO - 1)
    shape = (2 * group, lanes)
    lane_node = lax.broadcasted_iota(jnp.int32, shape, 1) % group
    sub = lax.broadcasted_iota(jnp.int32, shape, 0)
    mine = jnp.where(lane_node == sub % group, jnp.broadcast_to(high, shape) - sub // group, -100).astype(jnp.int8)
    one = jnp.ones(shape, F8)
    zero = jnp.zeros(shape, F8)
    left = jnp.concatenate([jnp.where(mine == jnp.int8(j), one, zero) for j in range(first, last, 2)], axis=0)
    lows = jnp.broadcast_to(low - 128, shape).astype(jnp.int8)
    right = jnp.concatenate(
        [jnp.where(lows == (sub + (j - 128)).astype(jnp.int8), one, zero) for j in range(0, LO, 2 * group)], axis=0
    )
    counts = lax.dot_general(left, right, (((1,), (1,)), ((), ())), preferred_element_type=F32)
    return counts.reshape(last - first, group, LO)


def group_rows(slot_ref, degree_ref, at, line, group):
    lane_slot = lax.broadcasted_iota(jnp.int32, (8, 128), 1) // group
    slot = lax.broadcasted_iota(jnp.int32, (8, 128), 0)
    parts = []
    for j in range(slot_ref.shape[0]):
        lines = jnp.where(slot + 8 * j < degree_ref[pl.ds(line, 1), :], slot_ref[j, at], -1)
        lines = pltpu.roll(lines, group, 1, stride=group, stride_axis=0)
        turned = jnp.zeros((8, 128), jnp.int32)
        for s in range(8):
            one = jnp.broadcast_to(lines[s : s + 1], (8, 128))
            turned = jnp.where(lane_slot == s, pltpu.roll(one, 0, 1, stride=group, stride_axis=0), turned)
        parts.append(turned)
    return jnp.concatenate(parts, axis=1)


def fill_counts(counts, index_ref, base, tile, group, first, last, beside=None):
    def pair(i, carry):
        both = [count_group(index_ref[pl.ds(base + ((2 * i + j) ^ 7), 1), :], group, first, last) for j in range(2)]
        both = jnp.concatenate(both, axis=1).astype(F8)
        at = pl.ds(pl.multiple_of(i * 2 * group, 2 * group), 2 * group)
        for h in range(last - first):
            counts[at, h * LO : (h + 1) * LO] = both[h]
        if beside is not None:
            beside(i)
        return carry

    lax.fori_loop(0, tile // (2 * group), pair, 0, unroll=UNROLL)


def own_kernel(
    slot_ref, degree_ref, most_ref, feat_ref, index_ref, table_ref, part_ref, inverse_ref,
    counts, feat, table, index, later, sems, *, tile, early, group, own
):
    nodes = feat.shape[0]
    lines = nodes // 128
    early_lines = early // 128
    last = early // tile - 1
    fetch = pltpu.make_async_copy(feat_ref, feat, sems.at[0])
    save_table = pltpu.make_async_copy(table, table_ref, sems.at[1])
    save_index = pltpu.make_async_copy(index, index_ref.at[pl.ds(0, early // group)], sems.at[2])
    save_later = pltpu.make_async_copy(later, index_ref.at[pl.ds(early // group, (nodes - early) // group)], sems.at[3])
    fetch.start()

    def relay(i, carry):
        index[pl.ds(pl.multiple_of(i * 8, 8), 8), :] = group_rows(slot_ref, degree_ref, i, i, group)
        return carry

    lax.fori_loop(0, early_lines, relay, 0, unroll=8)
    save_index.start()
    fetch.wait()

    scale, inverse_ref[...] = fit(most_ref[...])

    @pl.loop(0, nodes // 512)
    def _(i):
        at = pl.ds(pl.multiple_of(i * 512, 512), 512)
        table[at, :] = split(feat[at, :], scale[:1])

    save_table.start()

    @pl.loop(0, last + 1)
    def _(t):
        def relay_later(i):
            line = jnp.minimum(t * (tile // (2 * group)) + i, lines - early_lines - 1)
            rows = group_rows(slot_ref, degree_ref, early_lines + line, early_lines + line, group)
            later[pl.ds(pl.multiple_of(line * 8, 8), 8), :] = rows

        fill_counts(counts, index, t * (tile // group), tile, group, 0, own, relay_later)

        @pl.when(t == last)
        def _():
            save_later.start()

        total = jnp.dot(counts[...], table[...], preferred_element_type=F32)
        part_ref[pl.ds(pl.multiple_of(t * tile, tile), tile), :] = joined(total, inverse_ref[:1])

    save_index.wait()
    save_table.wait()
    save_later.wait()


def layer_kernel(
    index_ref, degree_ref, part_ref, own_inverse, feat_ref, halo_ref, table_ref, self_ref, neigh_ref, bias_ref, out_ref,
    table, counts, halo_inverse, halo, wide, hub_rows, sems, *, tile, early, group, peers, rows, hubs, own, highs
):
    nodes, width = table_ref.shape[0], feat_ref.shape[1]
    step = pl.program_id(0)
    block = rows + hubs
    own_copy = pltpu.make_async_copy(table_ref, table.at[pl.ds(0, nodes)], sems.at[0])
    halo_copy = pltpu.make_async_copy(halo_ref, halo, sems.at[1])

    @pl.when(step == 0)
    def _():
        halo_copy.start()
        own_copy.start()

    def add_halo():
        halo_copy.wait()
        wide[...] = halo[...].astype(F32)
        scale, halo_inverse[...] = fit(largest(wide[...]))
        hub_rows[...] = jnp.zeros_like(hub_rows)

        @pl.loop(0, peers, unroll=4)
        def _(i):
            at = pl.multiple_of(i * block, 8)
            table[pl.ds(pl.multiple_of(nodes + i * rows, 32), rows), :] = split(wide[pl.ds(at, rows), :], scale[:1])
            hub_rows[pl.ds(pl.multiple_of(i * hubs, 8), hubs), :] = wide[pl.ds(at + rows, hubs), :]

        table[nodes + peers * rows :, :] = split(hub_rows[...], scale[:1])

    def finish(total):
        eye = lax.broadcasted_iota(jnp.int32, (128, 128), 0) == lax.broadcasted_iota(jnp.int32, (128, 128), 1)
        ones = jnp.ones((128, width), BF16)
        spread = []
        for j in range(tile // 128):
            line = degree_ref[pl.ds(step * (tile // 128) + j, 1), :].astype(F32)
            spread.append(jnp.dot(jnp.where(eye, line, 0.0).astype(BF16), ones, preferred_element_type=F32))
        aggregate = (total / jnp.concatenate(spread, axis=0)).astype(BF16)
        mixed = jnp.dot(feat_ref[...], self_ref[...], preferred_element_type=F32)
        mixed = mixed + jnp.dot(aggregate, neigh_ref[...], preferred_element_type=F32) + bias_ref[...]
        out_ref[...] = jnp.maximum(mixed, 0.0).astype(BF16)

    @pl.when(step < early // tile)
    def _():
        fill_counts(counts, index_ref, 0, tile, group, own, highs)
        pl.when(step == 0)(add_halo)
        total = jnp.dot(counts[:, : (highs - own) * LO], table[own * LO :, :], preferred_element_type=F32)
        finish(joined(total, halo_inverse[:1]) + part_ref[...])

    @pl.when(step == early // tile)
    def _():
        own_copy.wait()

    @pl.when(step >= early // tile)
    def _():
        fill_counts(counts, index_ref, 0, tile, group, 0, highs)
        total = jnp.dot(counts[:, own * LO :], table[own * LO :, :], preferred_element_type=F32)
        total = joined(total, halo_inverse[:1])
        rest = jnp.dot(counts[:, : own * LO], table[: own * LO, :], preferred_element_type=F32)
        finish(total + joined(rest, own_inverse[:1]))


def local(features, neighbors, degree, send_list, hub_rows, w_self, w_neigh, bias):
    nodes, width = features.shape
    fanout = neighbors.shape[1]
    _, peers, rows = send_list.shape
    hubs = hub_rows.shape[1]
    block = rows + hubs
    group = 256 // fanout
    own = nodes // LO
    highs = -(-(nodes + peers * block) // (2 * LO)) * 2
    hub_space = highs * LO - nodes - peers * rows
    tile = TILE
    early = EARLY
    smem = pl.BlockSpec(memory_space=pltpu.SMEM)
    vmem = pl.BlockSpec(memory_space=pltpu.VMEM)
    params = pltpu.CompilerParams(vmem_limit_bytes=VMEM_BYTES)

    lines = neighbors.T.reshape(fanout // 8, 8, nodes // 128, 128).transpose(0, 2, 1, 3)
    degrees = degree.reshape(nodes // 128, 128)
    outgoing, most = pl.pallas_call(
        functools.partial(outgoing_kernel, peers=peers, rows=rows, hubs=hubs),
        in_specs=[smem, smem, vmem],
        out_specs=[vmem, vmem],
        out_shape=[jax.ShapeDtypeStruct((peers * block, width), BF16), jax.ShapeDtypeStruct((8, width), F32)],
        scratch_shapes=[pltpu.VMEM((nodes, width), F32), pltpu.VMEM((peers * block, width), F32)],
        compiler_params=params,
        name="outgoing_rows",
    )(send_list.reshape(-1), hub_rows.reshape(-1), features)
    halo = lax.all_to_all(outgoing.reshape(peers, block, width), "node", split_axis=0, concat_axis=0, tiled=True)
    halo = halo.reshape(peers * block, width)

    index, table, part, inverse = pl.pallas_call(
        functools.partial(own_kernel, tile=tile, early=early, group=group, own=own),
        grid=(1,),
        in_specs=[
            pl.BlockSpec((fanout // 8, nodes // 128, 8, 128), lambda i: (0, 0, 0, 0)),
            pl.BlockSpec((nodes // 128, 128), lambda i: (0, 0)),
            pl.BlockSpec((8, width), lambda i: (0, 0)),
            pl.BlockSpec(memory_space=pl.ANY),
        ],
        out_specs=[
            pl.BlockSpec(memory_space=pl.ANY),
            pl.BlockSpec(memory_space=pl.ANY),
            pl.BlockSpec((early, width), lambda i: (0, 0)),
            pl.BlockSpec((8, width), lambda i: (0, 0)),
        ],
        out_shape=[
            jax.ShapeDtypeStruct((nodes // group, group * fanout), jnp.int32),
            jax.ShapeDtypeStruct((nodes, 2 * width), F8),
            jax.ShapeDtypeStruct((early, width), F32),
            jax.ShapeDtypeStruct((8, width), F32),
        ],
        scratch_shapes=[
            pltpu.VMEM((tile, own * LO), F8),
            pltpu.VMEM((nodes, width), BF16),
            pltpu.VMEM((nodes, 2 * width), F8),
            pltpu.VMEM((early // group, group * fanout), jnp.int32),
            pltpu.VMEM(((nodes - early) // group, group * fanout), jnp.int32),
            pltpu.SemaphoreType.DMA((4,)),
        ],
        compiler_params=params,
        cost_estimate=pl.CostEstimate(flops=30_000_000_000, bytes_accessed=6_000_000, transcendentals=0),
        name="own_part",
    )(lines, degrees, most, features)

    whole = lambda *shape: pl.BlockSpec(shape, lambda i: (0,) * len(shape))
    last_early = early // tile - 1
    return pl.pallas_call(
        functools.partial(
            layer_kernel, tile=tile, early=early, group=group, peers=peers, rows=rows, hubs=hubs, own=own, highs=highs
        ),
        grid=(nodes // tile,),
        in_specs=[
            pl.BlockSpec((tile // group, group * fanout), lambda i: (i, 0)),
            whole(nodes // 128, 128),
            pl.BlockSpec((tile, width), lambda i: (jnp.minimum(i, last_early), 0)),
            whole(8, width),
            pl.BlockSpec((tile, width), lambda i: (i, 0)),
            pl.BlockSpec(memory_space=pl.ANY),
            pl.BlockSpec(memory_space=pl.ANY),
            whole(width, width),
            whole(width, width),
            whole(1, width),
        ],
        out_specs=pl.BlockSpec((tile, width), lambda i: (i, 0)),
        out_shape=jax.ShapeDtypeStruct((nodes, width), BF16),
        scratch_shapes=[
            pltpu.VMEM((highs * LO, 2 * width), F8),
            pltpu.VMEM((tile, highs * LO), F8),
            pltpu.VMEM((8, width), F32),
            pltpu.VMEM((peers * block, width), BF16),
            pltpu.VMEM((peers * block, width), F32),
            pltpu.VMEM((hub_space, width), F32),
            pltpu.SemaphoreType.DMA((2,)),
        ],
        compiler_params=params,
        name="sage_layer",
    )(index, degrees, part, inverse, features, halo, table, w_self, w_neigh, bias.reshape(1, width))


def solution(mesh):
    in_specs = (
        P(("groups", "node"), None),
        P(("groups", "node"), None),
        P(("groups", "node")),
        P(("groups", "node"), None, None),
        P(("groups", "node"), None),
        P(),
        P(),
        P(),
    )
    out_specs = P(("groups", "node"), None)
    return jax.shard_map(local, mesh=mesh, in_specs=in_specs, out_specs=out_specs, check_vma=False)
```
